32 devices in a mesh: risk: 16 (over z, y, x), tcol: 2 (over core).
Axes of the slice: x: 2, y: 2, z: 4, core: 2. Of those that a mesh axis runs over, the one named last changes fastest.
Arguments:
- idio_normals: bfloat16 [128, 131072], P('tcol', 'risk'), may hold values from -6 to 6
- factor_normals: bfloat16 [128, 64], P('tcol'), may hold values from -6 to 6
- loadings: bfloat16 [64, 131072], P(None, 'risk'), may hold values from -0.75 to 0.75
- log_scale: float32 [131072], P('risk'), may hold values from -1.5 to 0
- sigma: float32 [131072], P('risk'), may hold values from 0.2 to 0.7
- idio_weight: float32 [131072], P('risk'), may hold values from 0.3 to 1
- risk_slot: int32 [131072], P('risk'), may hold values from 0 to 127
- tile_owner: int32 [1024, 1], P('risk'), may hold values from 0 to 15; in each aligned block of 64 rows (0 to 63, 64 to 127, ...) at most 8 rows name the same one
- tile_sub: int32 [1024], P('risk'), may hold values from 0 to 5
- attach: float32 [12288], P('risk'), may hold values from 2 to 16
- limit: float32 [12288], P('risk'), may hold values from 2 to 20
- share_values: bfloat16 [96, 2, 128, 128], P('risk', None, 'tcol'), may hold values from 0 to 0.0012969971
- share_rblock: int32 [96, 2], P('risk'), may hold values from 0 to 3, all different within a row
Outputs:
- ceded_loss: float32 [128, 12288], P('tcol', 'risk')
- reinsurer_loss: float32 [128, 512], P('tcol', 'risk')
The draws below stay inside these ranges and needn't reach their ends.
Inputs may be any that keep to these rules, and one draw needn't show every extreme that they name: `tile_owner`: among the 64 tiles of one index of risk no owner is named more than 8 times, a bound that some block reaches. `share_rblock`: the 2 tiles of one treaty block name distinct reinsurer blocks.
All inputs are finite; a program needn't handle non-finite values.
Results may differ from the reference program's by a relative error of at most 0.0019.
Values may be sent and summed in bfloat16 or wider, within the bound.
No kernel may reach another device: no remote copies, remote signals or barrier semaphores. Data moves between devices by JAX's collectives and lax.ppermute only.
A program may use at most 64 MiB of HBM per device.

```python
import math
import jax
import jax.numpy as jnp
import numpy as np
from jax import lax

F = 64
TB = 128
TR = 128
BLK_OWN = 6
RB = 128
REINS = 512
KS = 2
TILES_DEV = 64
YEARS = 128
TILES = 1024
RISKS = 131072
TBLK = 96
TREATIES = 12288
CAP = 8
N_RISK = 16


def set_ends(values, stream_key, low, largest):
    place = [jax.random.randint(jax.random.fold_in(stream_key, axis), (), 0, length) for axis, length in enumerate(values.shape)]
    longest = values.shape.index(max(values.shape))
    next_to = place[:longest] + [(place[longest] + 1) % values.shape[longest]] + place[longest + 1:]
    return values.at[tuple(place)].set(low).at[tuple(next_to)].set(largest)


def shard_levels(key, shape, pieces, smallest, largest):
    gain = 1.0
    for axis_at, parts in pieces:
        heights = jax.random.uniform(jax.random.fold_in(jax.random.fold_in(key, 6), axis_at), (parts,), jnp.float32, smallest / len(pieces), largest / len(pieces))
        gain = gain * jnp.repeat(jnp.exp(heights), shape[axis_at] // parts).reshape((-1,) + (1,) * (len(shape) - 1 - axis_at))
    return gain


def choose_distinct(rng, rows, count, top, lift):
    order = jax.random.permutation(jax.random.fold_in(rng, 1), count)
    boost = order
    for power in range(3):
        boost = boost * boost // count
    boost = boost * lift // count
    chance = jax.random.randint(jax.random.fold_in(rng, 2), (rows, count), 0, 4096) + boost
    fixed_rows = jax.random.permutation(jax.random.fold_in(rng, 3), rows)[jnp.arange(count) % rows]
    chance = jnp.where(jnp.arange(rows)[:, None] == fixed_rows[None, :], 1 << 14, chance)
    merit = chance * count + jnp.arange(count)
    return lax.top_k(merit.astype(jnp.int32), top)[1].astype(jnp.int32)


def shared_out(rng, own, number, rows, number_of, top, reach, slope):
    ranking = jax.random.permutation(rng, number_of)
    packed, usual = portions_of(number_of, rows * top, reach, slope, True), portions_of(number_of, rows * top, reach, slope, False)
    places = jnp.arange(number_of)

    def named(tallies, offset_by):
        used = int((tallies > 0).sum())
        fixed = max(1, used // 4)
        shifted = fixed + (places - fixed + offset_by * (used - fixed)) % max(1, number_of - fixed)
        return jnp.zeros((number_of,), jnp.int32).at[ranking[jnp.where(places < fixed, places, shifted)]].set(jnp.asarray(tallies, jnp.int32))

    tallies = jnp.where(number % 4 == 0, named(packed, number // 4), named(usual, number - number // 4 - 1))
    mixed = jax.random.permutation(jax.random.fold_in(own, 3), number_of)
    donor, receiver = mixed[0:number_of // 2 * 2:2], mixed[1:number_of // 2 * 2:2]
    slack = jnp.minimum(tallies[donor] - 1, reach - tallies[receiver]) // 2
    slack = jnp.where((donor == ranking[0]) | (receiver == ranking[0]) | (tallies[receiver] == 0), 0, jnp.maximum(slack, 0))
    shifted = jax.random.randint(jax.random.fold_in(own, 4), (number_of // 2,), 0, 1 << 20) % (slack + 1)
    tallies = tallies.at[donor].add(-shifted).at[receiver].add(shifted)
    labels = jnp.searchsorted(jnp.cumsum(tallies), jnp.arange(rows * top), side="right").astype(jnp.int32)
    table = labels.reshape(top, rows).T
    table = table[jax.random.permutation(jax.random.fold_in(own, 1), rows)]
    offset_by = jax.random.randint(jax.random.fold_in(own, 2), (rows, 1), 0, top)
    return jnp.take_along_axis(table, (jnp.arange(top)[None, :] + offset_by) % top, axis=1)


def portions_of(number_of, total, most, lean, full):
    portions = [(1 << 20) // math.isqrt(standing ** lean) + 1 for standing in range(1, number_of + 1)]
    largest = most if full else min(most, max(-(-total // number_of), total * portions[0] // sum(portions)))
    least = 1 if total - largest >= number_of - 1 else 0
    given, surplus = [largest] + [least] * (number_of - 1), total - largest - least * (number_of - 1)
    while surplus > 0:
        free = [i for i in range(1, number_of) if given[i] < largest] or [i for i in range(1, number_of) if given[i] < most]
        whole, left = sum([portions[i] for i in free]), surplus
        for i in free:
            more = min(most - given[i], max(1, left * portions[i] // whole), surplus)
            given[i] = given[i] + more
            surplus = surplus - more
    return np.array(given)


def scatter_about(key, dims, scale, most, pieces=(), held_as=jnp.bfloat16):
    array = scale * jax.random.normal(key, dims, jnp.float32)
    if pieces:
        array = array * shard_levels(key, dims, pieces, -0.22, 0.18)
    return jnp.clip(array, -most, most).astype(held_as)


def setup_inputs(seed: int = 0) -> dict:
    splits = jax.random.split(jax.random.key(seed), 14)
    idio_normals = scatter_about(splits[0], (YEARS, RISKS), 1.0, 6.0, ((0, 2), (1, 16)))
    factor_normals = scatter_about(splits[1], (YEARS, F), 1.0, 6.0, ((0, 2),))
    loadings = scatter_about(splits[2], (F, RISKS), F ** -0.5, 0.75, ((1, 16),))
    log_scale = jnp.clip(-1.5 + 1.5 * jax.random.uniform(splits[3], (RISKS,), jnp.float32) ** shard_levels(splits[3], (RISKS,), ((0, 16),), -0.2, 0.2), -1.5, 0.0)
    sigma = jnp.clip(jnp.exp(math.log(0.7) - 1.2527629 * jax.random.uniform(splits[4], (RISKS,), jnp.float32) ** shard_levels(splits[4], (RISKS,), ((0, 16),), -0.2, 0.2)), 0.2, 0.7)
    idio_weight = jnp.clip(0.3 + 0.7 * jax.random.uniform(splits[5], (RISKS,), jnp.float32) ** shard_levels(splits[5], (RISKS,), ((0, 16),), -0.2, 0.2), 0.3, 1.0)
    risk_slot = set_ends(jax.random.randint(splits[6], (RISKS,), 0, TB), jax.random.fold_in(splits[6], 1), 0, TB - 1).astype(jnp.int32)
    tile_owner_keys = jax.random.split(jax.random.fold_in(splits[7], 1), TILES // TILES_DEV)
    tile_owner_turns = jax.random.permutation(jax.random.fold_in(splits[7], 3), TILES // TILES_DEV)
    tile_owner = jax.vmap(lambda own, number: shared_out(jax.random.fold_in(splits[7], 2), own, number, TILES_DEV, N_RISK, 1, CAP, 2))(tile_owner_keys, tile_owner_turns).reshape((TILES, 1))
    tile_sub = set_ends(jax.random.randint(splits[8], (TILES,), 0, BLK_OWN), jax.random.fold_in(splits[8], 1), 0, BLK_OWN - 1).astype(jnp.int32)
    attach = jnp.clip(jnp.exp(math.log(16.0) - 2.0794415 * jax.random.uniform(splits[9], (TREATIES,), jnp.float32) ** shard_levels(splits[9], (TREATIES,), ((0, 16),), -0.2, 0.2)), 2.0, 16.0)
    limit = jnp.clip(jnp.exp(math.log(20.0) - 2.3025851 * jax.random.uniform(splits[10], (TREATIES,), jnp.float32) ** shard_levels(splits[10], (TREATIES,), ((0, 16),), -0.2, 0.2)), 2.0, 20.0)
    share_values = jnp.clip(0.0012969971 * jax.random.uniform(splits[11], (TBLK, KS, TB, RB), jnp.float32) ** shard_levels(splits[11], (TBLK, KS, TB, RB), ((0, 16), (2, 2)), -0.2, 0.2), 0.0, 0.0012969971).astype(jnp.bfloat16)
    share_rblock = choose_distinct(splits[12], TBLK, REINS // RB, KS, 0)
    return {"idio_normals": idio_normals, "factor_normals": factor_normals, "loadings": loadings, "log_scale": log_scale, "sigma": sigma, "idio_weight": idio_weight, "risk_slot": risk_slot, "tile_owner": tile_owner, "tile_sub": tile_sub, "attach": attach, "limit": limit, "share_values": share_values, "share_rblock": share_rblock}


def reference(idio_normals, factor_normals, loadings, log_scale, sigma, idio_weight, risk_slot, tile_owner, tile_sub, attach, limit, share_values, share_rblock):
    risk_dev = TILES_DEV * TR
    block_ids = (tile_owner[:, 0] * BLK_OWN + tile_sub).astype(jnp.int32)

    def accumulate(index, gross):
        offset = (index * risk_dev).astype(jnp.int32)
        noise = lax.dynamic_slice_in_dim(idio_normals, offset, risk_dev, 1)
        loads = lax.dynamic_slice_in_dim(loadings, offset, risk_dev, 1)
        scales = lax.dynamic_slice_in_dim(log_scale, offset, risk_dev, 0)
        spread = lax.dynamic_slice_in_dim(sigma, offset, risk_dev, 0)
        weights = lax.dynamic_slice_in_dim(idio_weight, offset, risk_dev, 0)
        slots = lax.dynamic_slice_in_dim(risk_slot, offset, risk_dev, 0)
        blocks = lax.dynamic_slice_in_dim(block_ids, (index * TILES_DEV).astype(jnp.int32), TILES_DEV, 0)
        common = jnp.dot(factor_normals, loads, preferred_element_type=jnp.float32)
        latent = common + weights * noise.astype(jnp.float32)
        losses = jnp.exp(scales + spread * latent).astype(jnp.bfloat16)
        onehot = (slots.reshape(TILES_DEV, TR)[:, :, None] == jnp.arange(TB, dtype=jnp.int32)[None, None, :]).astype(jnp.float32)
        partials = jnp.einsum('ykr,krb->kyb', losses.astype(jnp.float32).reshape(YEARS, TILES_DEV, TR), onehot)
        return gross.at[blocks].add(partials)

    gross = lax.fori_loop(0, N_RISK, accumulate, jnp.zeros((TBLK, YEARS, TB), jnp.float32))
    gross = jnp.transpose(gross, (1, 0, 2)).reshape(YEARS, TREATIES)
    ceded_loss = jnp.minimum(jnp.maximum(gross - attach[None, :], 0.0), limit[None, :])
    ceded_low = ceded_loss.astype(jnp.bfloat16)
    selector = (share_rblock[:, :, None] == jnp.arange(REINS // RB, dtype=jnp.int32)[None, None, :]).astype(jnp.float32)
    shares = jnp.einsum('gkr,gktj->gtrj', selector, share_values.astype(jnp.float32))
    shares = shares.astype(jnp.bfloat16).reshape(TREATIES, REINS)
    reinsurer_loss = jnp.dot(ceded_low, shares, preferred_element_type=jnp.float32)
    return ceded_loss, reinsurer_loss
```

```python
import jax
import jax.numpy as jnp
from jax import lax
from jax.experimental import pallas as pl
from jax.experimental.pallas import tpu as pltpu
from jax.sharding import PartitionSpec as P

TB = 128
RB = 128
REINS = 512
TOP = 40.0
SCALE = 65535.0 / TOP
HALF = 32768


def encode(sums):
    steps = jnp.minimum(sums * SCALE + 0.5, 65535.0).astype(jnp.int32) - HALF
    return steps.astype(jnp.int16)


def decode(coded):
    return (coded.astype(jnp.int32) + HALF).astype(jnp.float32) * (1.0 / SCALE)


def block_sums_kernel(
    owner_ref, sub_ref, idio_ref, factor_ref, loads_ref, scale_ref, sigma_ref, weight_ref, slot_ref,
    out_ref, acc_ref,
):
    blocks_owned = acc_ref.shape[0] // lax.axis_size("risk")
    step = pl.program_id(0)
    tiles = scale_ref.shape[0]

    @pl.when(step == 0)
    def _():
        acc_ref[...] = jnp.zeros_like(acc_ref)

    factor = factor_ref[...]
    rows = lax.broadcasted_iota(jnp.int32, (TB, TB), 0)
    for k in range(tiles):
        cols = pl.ds(k * TB, TB)
        common = jnp.dot(factor, loads_ref[:, cols], preferred_element_type=jnp.float32)
        latent = common + weight_ref[pl.ds(k, 1), :] * idio_ref[:, cols].astype(jnp.float32)
        losses = jnp.exp(scale_ref[pl.ds(k, 1), :] + sigma_ref[pl.ds(k, 1), :] * latent)
        chosen = (rows == slot_ref[pl.ds(k, 1), :]).astype(jnp.float32).astype(jnp.bfloat16)
        sums = lax.dot_general(
            losses.astype(jnp.bfloat16), chosen, (((1,), (1,)), ((), ())),
            preferred_element_type=jnp.float32,
        )
        tile = step * tiles + k
        at = owner_ref[tile] * blocks_owned + sub_ref[tile]
        acc_ref[at] += sums

    @pl.when(step == pl.num_programs(0) - 1)
    def _():
        def body(b, carry):
            out_ref[b] = encode(acc_ref[b])
            return carry

        lax.fori_loop(0, acc_ref.shape[0], body, 0, unroll=4)


def block_sums(idio, factor, loads, log_scale, sigma, weight, slot, owner, sub, blocks, steps=4):
    years, risks = idio.shape
    tiles = sub.shape[0]
    per = tiles // steps
    fold = lambda a: a.reshape(tiles, TB)
    row = pl.BlockSpec((per, TB), lambda i: (i, 0))
    smem = pl.BlockSpec(memory_space=pltpu.SMEM)
    return pl.pallas_call(
        block_sums_kernel,
        grid=(steps,),
        in_specs=[
            smem,
            smem,
            pl.BlockSpec((years, per * TB), lambda i: (0, i)),
            pl.BlockSpec(factor.shape, lambda i: (0, 0)),
            pl.BlockSpec((loads.shape[0], per * TB), lambda i: (0, i)),
            row,
            row,
            row,
            row,
        ],
        out_specs=pl.BlockSpec((blocks, years, TB), lambda i: (0, 0, 0)),
        out_shape=jax.ShapeDtypeStruct((blocks, years, TB), jnp.int16),
        scratch_shapes=[pltpu.VMEM((blocks, years, TB), jnp.float32)],
        compiler_params=pltpu.CompilerParams(vmem_limit_bytes=40 * 2**20),
    )(owner.reshape(-1), sub, idio, factor, loads, fold(log_scale), fold(sigma), fold(weight), fold(slot))


def retro_kernel(rblock_ref, inbound_ref, attach_ref, limit_ref, mine_ref, other_ref, ceded_ref, out_ref, acc_ref):
    sources, owned, years, _ = inbound_ref.shape
    tiles = mine_ref.shape[1]
    first = lax.axis_index("tcol") == 0
    acc_ref[...] = jnp.zeros_like(acc_ref)
    for g in range(owned):
        gross = decode(inbound_ref[0, g])
        for s in range(1, sources):
            gross += decode(inbound_ref[s, g])
        ceded = jnp.minimum(jnp.maximum(gross - attach_ref[pl.ds(g, 1), :], 0.0), limit_ref[pl.ds(g, 1), :])
        ceded_ref[:, pl.ds(g * TB, TB)] = ceded
        low = ceded.astype(jnp.bfloat16)
        for k in range(tiles):
            mine, other = mine_ref[g, k], other_ref[g, k]
            top = jnp.where(first, mine, other)
            bottom = jnp.where(first, other, mine)
            part = jnp.dot(low, jnp.concatenate([top, bottom], axis=0), preferred_element_type=jnp.float32)
            acc_ref[rblock_ref[g, k]] += part
    wide = RB // 4
    quarter = years // 4
    lane = lax.broadcasted_iota(jnp.int32, (quarter, RB), 1) // wide
    for q in range(acc_ref.shape[0]):
        parts = [acc_ref[q, pl.ds(j * quarter, quarter), :] for j in range(4)]
        for i in range(4):
            packed = parts[i]
            for j in range(4):
                if j != i:
                    moved = pltpu.roll(parts[j], ((j - i) * wide) % RB, 1)
                    packed = jnp.where(lane == j, moved, packed)
            out_ref[4 * q + i] = packed


def retro(inbound, attach, limit, mine, other, rblock):
    sources, owned, years, _ = inbound.shape
    vmem = pl.BlockSpec(memory_space=pltpu.VMEM)
    return pl.pallas_call(
        retro_kernel,
        in_specs=[pl.BlockSpec(memory_space=pltpu.SMEM)] + [vmem] * 5,
        out_specs=[vmem, vmem],
        out_shape=[
            jax.ShapeDtypeStruct((years, owned * TB), jnp.float32),
            jax.ShapeDtypeStruct((REINS * 4 // RB, years // 4, RB), jnp.float32),
        ],
        scratch_shapes=[pltpu.VMEM((REINS // RB, years, RB), jnp.float32)],
        compiler_params=pltpu.CompilerParams(vmem_limit_bytes=40 * 2**20),
    )(rblock, inbound, attach.reshape(owned, TB), limit.reshape(owned, TB), mine, other)


def finish_kernel(in_ref, out_ref):
    total = in_ref[0]
    for s in range(1, in_ref.shape[0]):
        total += in_ref[s]
    quarter, wide = total.shape[0], RB // 4
    for j in range(4):
        out_ref[pl.ds(j * quarter, quarter), :] = total[:, j * wide : (j + 1) * wide]


def finish(pieces):
    return pl.pallas_call(
        finish_kernel,
        out_shape=jax.ShapeDtypeStruct((pieces.shape[1] * 4, RB // 4), jnp.float32),
    )(pieces)


def dense_on_device(
    idio_normals, factor_normals, loadings, log_scale, sigma, idio_weight, risk_slot,
    tile_owner, tile_sub, attach, limit, share_values, share_rblock,
):
    risk_count = lax.axis_size("risk")
    years_dev = idio_normals.shape[0]
    owned = attach.shape[0] // TB
    other_shares = lax.ppermute(share_values, "tcol", [(0, 1), (1, 0)])
    outbound = block_sums(
        idio_normals, factor_normals, loadings, log_scale, sigma, idio_weight, risk_slot,
        tile_owner, tile_sub, risk_count * owned,
    )
    inbound = lax.all_to_all(outbound, "risk", split_axis=0, concat_axis=0, tiled=True)
    inbound = inbound.reshape(risk_count, owned, years_dev, TB)
    ceded, pieces = retro(inbound, attach, limit, share_values, other_shares, share_rblock)
    pieces = lax.all_to_all(pieces, "risk", split_axis=0, concat_axis=0, tiled=True)
    return ceded, finish(pieces)


def sparse_on_device(
    idio_normals, factor_normals, loadings, log_scale, sigma, idio_weight, risk_slot,
    tile_owner, tile_sub, attach, limit, share_values, share_rblock,
):
    risk_count = lax.axis_size("risk")
    years_dev, risk_dev = idio_normals.shape
    tile_count = tile_sub.shape[0]
    tile_rows = risk_dev // tile_count
    blocks_owned = attach.shape[0] // TB
    common = jnp.dot(factor_normals, loadings, preferred_element_type=jnp.float32)
    latent = common + idio_weight * idio_normals.astype(jnp.float32)
    losses = jnp.exp(log_scale + sigma * latent).astype(jnp.bfloat16)
    onehot = (
        risk_slot.reshape(tile_count, tile_rows)[:, :, None]
        == jnp.arange(TB, dtype=jnp.int32)[None, None, :]
    ).astype(jnp.bfloat16)
    partials = jnp.einsum(
        "ykr,krb->kyb",
        losses.reshape(years_dev, tile_count, tile_rows),
        onehot,
        preferred_element_type=jnp.float32,
    )
    owners = tile_owner[:, 0]
    capacity = 2 * tile_count // risk_count
    matches = owners[:, None] == owners[None, :]
    earlier = jnp.arange(tile_count)[None, :] < jnp.arange(tile_count)[:, None]
    position = jnp.sum(jnp.logical_and(matches, earlier), axis=1)
    slot_id = owners * capacity + position
    outbound = (
        jnp.zeros((risk_count * capacity, years_dev, TB), jnp.float32).at[slot_id].set(partials)
    )
    outbound = outbound.reshape(risk_count, capacity, years_dev, TB)
    sub_ids = (
        jnp.zeros((risk_count * capacity,), jnp.float32)
        .at[slot_id]
        .set(tile_sub.astype(jnp.float32))
    )
    sub_ids = sub_ids.reshape(risk_count, capacity)
    inbound, inbound_ids = (
        lax.all_to_all(outbound, "risk", split_axis=0, concat_axis=0, tiled=True),
        lax.all_to_all(sub_ids, "risk", split_axis=0, concat_axis=0, tiled=True),
    )
    selector = (
        inbound_ids.reshape(-1)[:, None] == jnp.arange(blocks_owned, dtype=jnp.float32)[None, :]
    ).astype(jnp.float32)
    gross = jnp.einsum(
        "sg,syb->ygb", selector, inbound.reshape(-1, years_dev, TB), precision=lax.Precision.HIGHEST
    )
    ceded = jnp.minimum(
        jnp.maximum(gross - attach.reshape(1, blocks_owned, TB), 0.0),
        limit.reshape(1, blocks_owned, TB),
    )
    ceded_low = ceded.astype(jnp.bfloat16)
    rein_blocks = REINS // RB
    selector_low = (
        share_rblock[:, :, None] == jnp.arange(rein_blocks, dtype=jnp.int32)[None, None, :]
    ).astype(jnp.bfloat16)
    shares = lax.all_gather(share_values, "tcol", axis=2, tiled=True)
    count_rows = shares.shape[2]
    spread = jnp.einsum("gkr,gktj->gtrj", selector_low, shares, preferred_element_type=jnp.float32)
    spread = spread.astype(jnp.bfloat16).reshape(blocks_owned, count_rows, REINS)
    retro_terms = jnp.einsum("ygt,gtr->yr", ceded_low, spread, preferred_element_type=jnp.float32)
    reinsurer_loss = lax.psum_scatter(retro_terms, "risk", scatter_dimension=1, tiled=True)
    return (ceded.reshape(years_dev, blocks_owned * TB), reinsurer_loss)


def solution(mesh):
    placed = (
        P("tcol", "risk"),
        P("tcol", None),
        P(None, "risk"),
        P("risk"),
        P("risk"),
        P("risk"),
        P("risk"),
        P("risk", None),
        P("risk"),
        P("risk"),
        P("risk"),
        P("risk", None, "tcol", None),
        P("risk", None),
    )
    dense = mesh.shape["risk"] == 4 * REINS // RB and mesh.shape["tcol"] == 2
    return jax.shard_map(
        dense_on_device if dense else sparse_on_device,
        mesh=mesh,
        in_specs=placed,
        out_specs=(P("tcol", "risk"), P("tcol", "risk")),
        check_vma=False,
    )
```

```python
import functools

import jax
import jax.numpy as jnp
from jax import lax
from jax.experimental import pallas as pl
from jax.experimental.pallas import tpu as pltpu
from jax.sharding import PartitionSpec as P

TB = 128
RB = 128
REINS = 512
TOP = 40.0
SCALE = 65535.0 / TOP
HALF = 32768


def encode(sums):
    steps = jnp.minimum(sums * SCALE + 0.5, 65535.0).astype(jnp.int32) - HALF
    return steps.astype(jnp.int16)


def decode(coded):
    return (coded.astype(jnp.int32) + HALF).astype(jnp.float32) * (1.0 / SCALE)


def relative_code(rel, order):
    code = 0
    for bit in order:
        code = code * 2 + ((rel >> bit) & 1)
    return code


def block_sums_kernel(
    parts, owned, owner_ref, sub_ref, idio_ref, factor_ref, loads_ref, scale_ref, sigma_ref, weight_ref, slot_ref,
    *out_refs,
):
    send_refs, keep_refs, high_refs = (out_refs[i * len(parts) : (i + 1) * len(parts)] for i in range(3))
    half = keep_refs[0].shape[0]
    step = pl.program_id(0)
    tiles = scale_ref.shape[0]
    me = lax.axis_index("risk")
    core = lax.axis_index("tcol")

    @pl.when(step == 0)
    def _():
        for ref in keep_refs + high_refs:
            ref[...] = jnp.zeros_like(ref)

    factor = factor_ref[...]
    rows = lax.broadcasted_iota(jnp.int32, (TB, TB), 0)
    for k in range(tiles):
        cols = pl.ds(k * TB, TB)
        common = jnp.dot(factor, loads_ref[:, cols], preferred_element_type=jnp.float32)
        latent = common + weight_ref[pl.ds(k, 1), :] * idio_ref[:, cols].astype(jnp.float32)
        losses = jnp.exp(scale_ref[pl.ds(k, 1), :] + sigma_ref[pl.ds(k, 1), :] * latent)
        chosen = (rows == slot_ref[pl.ds(k, 1), :]).astype(jnp.float32).astype(jnp.bfloat16)
        sums = lax.dot_general(
            losses.astype(jnp.bfloat16), chosen, (((1,), (1,)), ((), ())),
            preferred_element_type=jnp.float32,
        )
        tile = step * tiles + k
        rel = owner_ref[tile] ^ me
        for (first, count, order), keep_ref, high_ref in zip(parts, keep_refs, high_refs):
            code = jnp.where(core == 0, relative_code(rel, order[0]), relative_code(rel, order[1]))
            at = code * owned + sub_ref[tile]
            mine = sums[first : first + count]

            @pl.when(at < half)
            def _():
                keep_ref[at] += mine

            @pl.when(at >= half)
            def _():
                high_ref[at - half] += mine

    @pl.when(step == pl.num_programs(0) - 1)
    def _():
        for send_ref, high_ref in zip(send_refs, high_refs):

            def body(b, carry):
                send_ref[b] = encode(high_ref[b])
                return carry

            lax.fori_loop(0, half, body, 0, unroll=4)


def block_sums(parts, idio, factor, loads, log_scale, sigma, weight, slot, owner, sub, blocks, owned, steps=4):
    years, risks = idio.shape
    tiles = sub.shape[0]
    per = tiles // steps
    fold = lambda a: a.reshape(tiles, TB)
    row = pl.BlockSpec((per, TB), lambda i: (i, 0))
    smem = pl.BlockSpec(memory_space=pltpu.SMEM)
    shapes = [(blocks // 2, count, TB) for _, count, _ in parts]
    whole = [pl.BlockSpec(s, lambda i: (0, 0, 0)) for s in shapes]
    out = pl.pallas_call(
        functools.partial(block_sums_kernel, parts, owned),
        grid=(steps,),
        in_specs=[
            smem,
            smem,
            pl.BlockSpec((years, per * TB), lambda i: (0, i)),
            pl.BlockSpec(factor.shape, lambda i: (0, 0)),
            pl.BlockSpec((loads.shape[0], per * TB), lambda i: (0, i)),
            row,
            row,
            row,
            row,
        ],
        out_specs=whole * 2,
        out_shape=[jax.ShapeDtypeStruct(s, jnp.int16) for s in shapes]
        + [jax.ShapeDtypeStruct(s, jnp.float32) for s in shapes],
        scratch_shapes=[pltpu.VMEM(s, jnp.float32) for s in shapes],
        compiler_params=pltpu.CompilerParams(vmem_limit_bytes=60 * 2**20),
    )(owner.reshape(-1), sub, idio, factor, loads, fold(log_scale), fold(sigma), fold(weight), fold(slot))
    return out[: len(parts)], out[len(parts) :]


def retro_kernel(parts, rblock_ref, attach_ref, limit_ref, mine_ref, other_ref, *refs):
    *in_refs, ceded_ref, out_ref, acc_ref = refs
    each = len(in_refs) // len(parts)
    owned, tiles = mine_ref.shape[:2]
    first = lax.axis_index("tcol") == 0
    acc_ref[...] = jnp.zeros_like(acc_ref)
    for g in range(owned):
        sums = []
        for p in range(len(parts)):
            gross, *inbound = in_refs[p * each : (p + 1) * each]
            total = gross[g]
            for ref in inbound:
                total += decode(ref[g])
            sums.append(total)
        gross = jnp.concatenate(sums, axis=0)
        ceded = jnp.minimum(jnp.maximum(gross - attach_ref[pl.ds(g, 1), :], 0.0), limit_ref[pl.ds(g, 1), :])
        ceded_ref[:, pl.ds(g * TB, TB)] = ceded
        low = ceded.astype(jnp.bfloat16)
        for k in range(tiles):
            mine, other = mine_ref[g, k], other_ref[g, k]
            top = jnp.where(first, mine, other)
            bottom = jnp.where(first, other, mine)
            part = lax.dot_general(
                jnp.concatenate([top, bottom], axis=0), low, (((0,), (1,)), ((), ())),
                preferred_element_type=jnp.float32,
            )
            acc_ref[rblock_ref[g, k]] += part
    wide = RB // 4
    for q in range(acc_ref.shape[0]):
        for i in range(4):
            for h in range(2):
                out_ref[4 * q + i, :, h * 64 : (h + 1) * 64] = acc_ref[q, pl.ds(i * wide + h * wide // 2, wide // 2), :]


def retro(parts, inbound, attach, limit, mine, other, rblock):
    owned = mine.shape[0]
    years = sum(count for _, count, _ in parts)
    vmem = pl.BlockSpec(memory_space=pltpu.VMEM)
    whole = lambda a: pl.BlockSpec(a.shape, lambda i: (0,) * a.ndim)
    first = lambda a: pl.BlockSpec((owned,) + a.shape[1:], lambda i: (0, 0, 0))
    attach, limit = attach.reshape(owned, TB), limit.reshape(owned, TB)
    outs = [
        jax.ShapeDtypeStruct((years, owned * TB), jnp.float32),
        jax.ShapeDtypeStruct((REINS * 4 // RB, RB // 8, RB), jnp.float32),
    ]
    return pl.pallas_call(
        functools.partial(retro_kernel, parts),
        grid=(1,),
        in_specs=[pl.BlockSpec(memory_space=pltpu.SMEM)]
        + [whole(a) for a in (attach, limit, mine, other)]
        + [first(a) for a in inbound],
        out_specs=[whole(a) for a in outs],
        out_shape=outs,
        scratch_shapes=[pltpu.VMEM((REINS // RB, RB, years), jnp.float32)],
        compiler_params=pltpu.CompilerParams(vmem_limit_bytes=20 * 2**20),
    )(rblock, attach, limit, mine, other, *inbound)


def finish_kernel(in_ref, out_ref):
    total = in_ref[0]
    for s in range(1, in_ref.shape[0]):
        total += in_ref[s]
    half, years = out_ref.shape[0] // 2, out_ref.shape[1]
    for h in range(2):
        out_ref[pl.ds(h * half, half), :] = total[:, h * years : (h + 1) * years]


def finish(pieces):
    return pl.pallas_call(
        finish_kernel,
        out_shape=jax.ShapeDtypeStruct((RB // 4, 2 * RB // 4), jnp.float32),
    )(pieces).T


PARTS = ((0, 64, ((0, 1, 2, 3), (1, 0, 2, 3))),)


def dense_on_device(
    idio_normals, factor_normals, loadings, log_scale, sigma, idio_weight, risk_slot,
    tile_owner, tile_sub, attach, limit, share_values, share_rblock,
):
    risk_count = lax.axis_size("risk")
    owned = attach.shape[0] // TB
    other_shares = lax.ppermute(share_values, "tcol", [(0, 1), (1, 0)])
    sends, keeps = block_sums(
        PARTS, idio_normals, factor_normals, loadings, log_scale, sigma, idio_weight, risk_slot,
        tile_owner, tile_sub, risk_count * owned, owned,
    )
    received = [[keep] for keep in keeps]
    sends = list(sends)
    steps = len(PARTS[0][2][0])
    count = keeps[0].shape[0]
    for step in range(steps):
        for p, (_, _, order) in enumerate(PARTS):
            pairs = [
                (2 * r + c, 2 * (r ^ (1 << order[c][step])) + c) for r in range(risk_count) for c in range(2)
            ]
            received[p].append(lax.ppermute(sends[p], ("risk", "tcol"), pairs))
        if step < steps - 1:
            count //= 2
            for p in range(len(PARTS)):
                total, *inbound = [a[count : 2 * count] for a in received[p]]
                for a in inbound:
                    total += decode(a)
                sends[p] = encode(total)
    inbound = [a for arrays in received for a in arrays]
    ceded, pieces = retro(PARTS, inbound, attach, limit, share_values, other_shares, share_rblock)
    pieces = lax.all_to_all(pieces, "risk", split_axis=0, concat_axis=0, tiled=True)
    return ceded, finish(pieces)


def sparse_on_device(
    idio_normals, factor_normals, loadings, log_scale, sigma, idio_weight, risk_slot,
    tile_owner, tile_sub, attach, limit, share_values, share_rblock,
):
    risk_count = lax.axis_size("risk")
    years_dev, risk_dev = idio_normals.shape
    tile_count = tile_sub.shape[0]
    tile_rows = risk_dev // tile_count
    blocks_owned = attach.shape[0] // TB
    common = jnp.dot(factor_normals, loadings, preferred_element_type=jnp.float32)
    latent = common + idio_weight * idio_normals.astype(jnp.float32)
    losses = jnp.exp(log_scale + sigma * latent).astype(jnp.bfloat16)
    onehot = (
        risk_slot.reshape(tile_count, tile_rows)[:, :, None]
        == jnp.arange(TB, dtype=jnp.int32)[None, None, :]
    ).astype(jnp.bfloat16)
    partials = jnp.einsum(
        "ykr,krb->kyb",
        losses.reshape(years_dev, tile_count, tile_rows),
        onehot,
        preferred_element_type=jnp.float32,
    )
    owners = tile_owner[:, 0]
    capacity = 2 * tile_count // risk_count
    matches = owners[:, None] == owners[None, :]
    earlier = jnp.arange(tile_count)[None, :] < jnp.arange(tile_count)[:, None]
    position = jnp.sum(jnp.logical_and(matches, earlier), axis=1)
    slot_id = owners * capacity + position
    outbound = (
        jnp.zeros((risk_count * capacity, years_dev, TB), jnp.float32).at[slot_id].set(partials)
    )
    outbound = outbound.reshape(risk_count, capacity, years_dev, TB)
    sub_ids = (
        jnp.zeros((risk_count * capacity,), jnp.float32)
        .at[slot_id]
        .set(tile_sub.astype(jnp.float32))
    )
    sub_ids = sub_ids.reshape(risk_count, capacity)
    inbound, inbound_ids = (
        lax.all_to_all(outbound, "risk", split_axis=0, concat_axis=0, tiled=True),
        lax.all_to_all(sub_ids, "risk", split_axis=0, concat_axis=0, tiled=True),
    )
    selector = (
        inbound_ids.reshape(-1)[:, None] == jnp.arange(blocks_owned, dtype=jnp.float32)[None, :]
    ).astype(jnp.float32)
    gross = jnp.einsum(
        "sg,syb->ygb", selector, inbound.reshape(-1, years_dev, TB), precision=lax.Precision.HIGHEST
    )
    ceded = jnp.minimum(
        jnp.maximum(gross - attach.reshape(1, blocks_owned, TB), 0.0),
        limit.reshape(1, blocks_owned, TB),
    )
    ceded_low = ceded.astype(jnp.bfloat16)
    rein_blocks = REINS // RB
    selector_low = (
        share_rblock[:, :, None] == jnp.arange(rein_blocks, dtype=jnp.int32)[None, None, :]
    ).astype(jnp.bfloat16)
    shares = lax.all_gather(share_values, "tcol", axis=2, tiled=True)
    count_rows = shares.shape[2]
    spread = jnp.einsum("gkr,gktj->gtrj", selector_low, shares, preferred_element_type=jnp.float32)
    spread = spread.astype(jnp.bfloat16).reshape(blocks_owned, count_rows, REINS)
    retro_terms = jnp.einsum("ygt,gtr->yr", ceded_low, spread, preferred_element_type=jnp.float32)
    reinsurer_loss = lax.psum_scatter(retro_terms, "risk", scatter_dimension=1, tiled=True)
    return (ceded.reshape(years_dev, blocks_owned * TB), reinsurer_loss)


def solution(mesh):
    placed = (
        P("tcol", "risk"),
        P("tcol", None),
        P(None, "risk"),
        P("risk"),
        P("risk"),
        P("risk"),
        P("risk"),
        P("risk", None),
        P("risk"),
        P("risk"),
        P("risk"),
        P("risk", None, "tcol", None),
        P("risk", None),
    )
    dense = mesh.shape["risk"] == 4 * REINS // RB and mesh.shape["tcol"] == 2
    return jax.shard_map(
        dense_on_device if dense else sparse_on_device,
        mesh=mesh,
        in_specs=placed,
        out_specs=(P("tcol", "risk"), P("tcol", "risk")),
        check_vma=False,
    )
```

```python
import functools

import jax
import jax.numpy as jnp
from jax import lax
from jax.experimental import pallas as pl
from jax.experimental.pallas import tpu as pltpu
from jax.sharding import PartitionSpec as P

TB = 128
RB = 128
REINS = 512
TOP = 40.0
SCALE = 65535.0 / TOP
HALF = 32768
VMEM_SUMS = 56


def encode(sums):
    steps = jnp.minimum(sums * SCALE + 0.5, 65535.0).astype(jnp.int32) - HALF
    return steps.astype(jnp.int16)


def decode(*coded):
    return sum(a.astype(jnp.int32) + HALF for a in coded).astype(jnp.float32) * (1.0 / SCALE)


def add_coded(*coded):
    steps = sum(a.astype(jnp.int32) for a in coded) + (len(coded) - 1) * HALF
    return jnp.minimum(steps, HALF - 1).astype(jnp.int16)


def relative_code(rel, order):
    code = 0
    for bit in order:
        code = code * 2 + ((rel >> bit) & 1)
    return code


def block_sums_kernel(parts, owned, chunks, *refs):
    count = len(parts)
    in_refs, refs = refs[:9], refs[9:]
    send_refs, keep_refs, sum_refs, coded_refs = (refs[i * count : (i + 1) * count] for i in range(4))
    *held, small_sems, sems, out_sems = refs[4 * count :]
    owner_ref, sub_ref, factor_ref, scale_ref, sigma_ref, weight_ref, slot_ref, idio_ref, loads_ref = held
    half = keep_refs[0].shape[0]
    tiles = scale_ref.shape[0]
    per = tiles // chunks
    me = lax.axis_index("risk")
    core = lax.axis_index("tcol")

    def copies(i):
        cols = pl.ds(i * per * TB, per * TB)
        return [
            pltpu.make_async_copy(source.at[:, cols], target.at[:, cols], sems.at[j, i])
            for j, (source, target) in enumerate(zip(in_refs[7:], held[7:]))
        ]

    small = [
        pltpu.make_async_copy(source, target, small_sems.at[j])
        for j, (source, target) in enumerate(zip(in_refs[:7], held[:7]))
    ]
    for copy in small + [copy for i in range(chunks) for copy in copies(i)]:
        copy.start()
    for ref in sum_refs:
        ref[...] = jnp.zeros_like(ref)
    for copy in small:
        copy.wait()

    factor = factor_ref[...]
    rows = lax.broadcasted_iota(jnp.int32, (TB, TB), 0)

    for i in range(chunks):
        for copy in copies(i):
            copy.wait()
        for j in range(i * per, (i + 1) * per, GROUP):
            common = jnp.dot(factor, loads_ref[:, pl.ds(j * TB, GROUP * TB)], preferred_element_type=jnp.float32)
            group = []
            for k in range(j, j + GROUP):
                noise = idio_ref[:, pl.ds(k * TB, TB)].astype(jnp.float32)
                latent = common[:, (k - j) * TB : (k - j + 1) * TB] + weight_ref[pl.ds(k, 1), :] * noise
                losses = jnp.exp(scale_ref[pl.ds(k, 1), :] + sigma_ref[pl.ds(k, 1), :] * latent)
                group.append(losses.astype(jnp.bfloat16))
            for k, losses in zip(range(j, j + GROUP), group):
                chosen = (rows == slot_ref[pl.ds(k, 1), :]).astype(jnp.float32).astype(jnp.bfloat16)
                sums = lax.dot_general(
                    losses, chosen, (((1,), (1,)), ((), ())), preferred_element_type=jnp.float32
                )
                rel = owner_ref[k] ^ me
                for (first, years, order), sum_ref in zip(parts, sum_refs):
                    code = jnp.where(core == 0, relative_code(rel, order[0]), relative_code(rel, order[1]))
                    sum_ref[code * owned + sub_ref[k]] += sums[first : first + years]

    out = []
    piece = half // PIECES
    for i in range(PIECES):
        at = pl.ds(i * piece, piece)
        for p, (send_ref, keep_ref, sum_ref, coded_ref) in enumerate(zip(send_refs, keep_refs, sum_refs, coded_refs)):

            def body(b, carry):
                coded_ref[b] = encode(sum_ref[b])
                coded_ref[half + b] = encode(sum_ref[half + b])
                return carry

            lax.fori_loop(i * piece, (i + 1) * piece, body, 0, unroll=2)
            for j, (source, target) in enumerate(((coded_ref.at[pl.ds(half + i * piece, piece)], send_ref), (coded_ref.at[at], keep_ref))):
                copy = pltpu.make_async_copy(source, target.at[at], out_sems.at[p, i, j])
                copy.start()
                out.append(copy)
    for copy in out:
        copy.wait()


GROUP = 16
PIECES = 2


def block_sums(parts, idio, factor, loads, log_scale, sigma, weight, slot, owner, sub, blocks, owned, chunks=2):
    tiles = sub.shape[0]
    fold = lambda a: a.reshape(tiles, TB)
    hbm = pl.BlockSpec(memory_space=pltpu.HBM)
    shapes = [(blocks // 2, years, TB) for _, years, _ in parts]
    inputs = (owner.reshape(-1), sub, factor, fold(log_scale), fold(sigma), fold(weight), fold(slot), idio, loads)
    out = pl.pallas_call(
        functools.partial(block_sums_kernel, parts, owned, chunks),
        in_specs=[hbm] * len(inputs),
        out_specs=[hbm] * (2 * len(parts)),
        out_shape=[jax.ShapeDtypeStruct(s, jnp.int16) for s in shapes * 2],
        scratch_shapes=[pltpu.VMEM((blocks, years, TB), jnp.float32) for _, years, _ in parts]
        + [pltpu.VMEM((blocks, years, TB), jnp.int16) for _, years, _ in parts]
        + [pltpu.SMEM(a.shape, a.dtype) for a in inputs[:2]]
        + [pltpu.VMEM(a.shape, a.dtype) for a in inputs[2:]]
        + [
            pltpu.SemaphoreType.DMA((7,)),
            pltpu.SemaphoreType.DMA((2, chunks)),
            pltpu.SemaphoreType.DMA((len(parts), PIECES, 2)),
        ],
        compiler_params=pltpu.CompilerParams(vmem_limit_bytes=VMEM_SUMS * 2**20),
    )(*inputs)
    return out[: len(parts)], out[len(parts) :]


def retro_kernel(parts, rblock_ref, attach_ref, limit_ref, mine_ref, other_ref, *refs):
    *in_refs, ceded_ref, out_ref, acc_ref = refs
    each = len(in_refs) // len(parts)
    owned, tiles = mine_ref.shape[:2]
    first = lax.axis_index("tcol") == 0
    acc_ref[...] = jnp.zeros_like(acc_ref)
    for g in range(owned):
        sums = []
        for p in range(len(parts)):
            sums.append(decode(*(ref[g] for ref in in_refs[p * each : (p + 1) * each])))
        gross = jnp.concatenate(sums, axis=0)
        ceded = jnp.minimum(jnp.maximum(gross - attach_ref[pl.ds(g, 1), :], 0.0), limit_ref[pl.ds(g, 1), :])
        ceded_ref[:, pl.ds(g * TB, TB)] = ceded
        low = ceded.astype(jnp.bfloat16)
        for k in range(tiles):
            mine, other = mine_ref[g, k], other_ref[g, k]
            top = jnp.where(first, mine, other)
            bottom = jnp.where(first, other, mine)
            part = lax.dot_general(
                jnp.concatenate([top, bottom], axis=0), low, (((0,), (1,)), ((), ())),
                preferred_element_type=jnp.float32,
            )
            acc_ref[rblock_ref[g, k]] += part
    wide = RB // 4
    for q in range(acc_ref.shape[0]):
        for i in range(4):
            for h in range(2):
                out_ref[4 * q + i, :, h * 64 : (h + 1) * 64] = acc_ref[q, pl.ds(i * wide + h * wide // 2, wide // 2), :]


def retro(parts, inbound, attach, limit, mine, other, rblock):
    owned = mine.shape[0]
    years = sum(count for _, count, _ in parts)
    vmem = pl.BlockSpec(memory_space=pltpu.VMEM)
    whole = lambda a: pl.BlockSpec(a.shape, lambda i: (0,) * a.ndim)
    first = lambda a: pl.BlockSpec((owned,) + a.shape[1:], lambda i: (0, 0, 0))
    attach, limit = attach.reshape(owned, TB), limit.reshape(owned, TB)
    outs = [
        jax.ShapeDtypeStruct((years, owned * TB), jnp.float32),
        jax.ShapeDtypeStruct((REINS * 4 // RB, RB // 8, RB), jnp.float32),
    ]
    return pl.pallas_call(
        functools.partial(retro_kernel, parts),
        grid=(1,),
        in_specs=[pl.BlockSpec(memory_space=pltpu.SMEM)]
        + [whole(a) for a in (attach, limit, mine, other)]
        + [first(a) for a in inbound],
        out_specs=[whole(a) for a in outs],
        out_shape=outs,
        scratch_shapes=[pltpu.VMEM((REINS // RB, RB, years), jnp.float32)],
        compiler_params=pltpu.CompilerParams(vmem_limit_bytes=20 * 2**20),
    )(rblock, attach, limit, mine, other, *inbound)


def finish_kernel(in_ref, out_ref):
    total = in_ref[0]
    for s in range(1, in_ref.shape[0]):
        total += in_ref[s]
    half, years = out_ref.shape[0] // 2, out_ref.shape[1]
    for h in range(2):
        out_ref[pl.ds(h * half, half), :] = total[:, h * years : (h + 1) * years]


def finish(pieces):
    return pl.pallas_call(
        finish_kernel,
        out_shape=jax.ShapeDtypeStruct((RB // 4, 2 * RB // 4), jnp.float32),
    )(pieces).T


PARTS = ((0, 64, ((0, 1, 2, 3), (1, 0, 2, 3))),)


def dense_on_device(
    idio_normals, factor_normals, loadings, log_scale, sigma, idio_weight, risk_slot,
    tile_owner, tile_sub, attach, limit, share_values, share_rblock,
):
    risk_count = lax.axis_size("risk")
    owned = attach.shape[0] // TB
    other_shares = lax.ppermute(share_values, "tcol", [(0, 1), (1, 0)])
    sends, keeps = block_sums(
        PARTS, idio_normals, factor_normals, loadings, log_scale, sigma, idio_weight, risk_slot,
        tile_owner, tile_sub, risk_count * owned, owned,
    )
    received = [[keep] for keep in keeps]
    sends = list(sends)
    steps = len(PARTS[0][2][0])
    count = keeps[0].shape[0]
    for step in range(steps):
        for p, (_, _, order) in enumerate(PARTS):
            pairs = [
                (2 * r + c, 2 * (r ^ (1 << order[c][step])) + c) for r in range(risk_count) for c in range(2)
            ]
            received[p].append(lax.ppermute(sends[p], ("risk", "tcol"), pairs))
        if step < steps - 1:
            count //= 2
            for p in range(len(PARTS)):
                sends[p] = add_coded(*(a[count : 2 * count] for a in received[p]))
    inbound = [a for arrays in received for a in arrays]
    ceded, pieces = retro(PARTS, inbound, attach, limit, share_values, other_shares, share_rblock)
    pieces = lax.all_to_all(pieces, "risk", split_axis=0, concat_axis=0, tiled=True)
    return ceded, finish(pieces)


def sparse_on_device(
    idio_normals, factor_normals, loadings, log_scale, sigma, idio_weight, risk_slot,
    tile_owner, tile_sub, attach, limit, share_values, share_rblock,
):
    risk_count = lax.axis_size("risk")
    years_dev, risk_dev = idio_normals.shape
    tile_count = tile_sub.shape[0]
    tile_rows = risk_dev // tile_count
    blocks_owned = attach.shape[0] // TB
    common = jnp.dot(factor_normals, loadings, preferred_element_type=jnp.float32)
    latent = common + idio_weight * idio_normals.astype(jnp.float32)
    losses = jnp.exp(log_scale + sigma * latent).astype(jnp.bfloat16)
    onehot = (
        risk_slot.reshape(tile_count, tile_rows)[:, :, None]
        == jnp.arange(TB, dtype=jnp.int32)[None, None, :]
    ).astype(jnp.bfloat16)
    partials = jnp.einsum(
        "ykr,krb->kyb",
        losses.reshape(years_dev, tile_count, tile_rows),
        onehot,
        preferred_element_type=jnp.float32,
    )
    owners = tile_owner[:, 0]
    capacity = 2 * tile_count // risk_count
    matches = owners[:, None] == owners[None, :]
    earlier = jnp.arange(tile_count)[None, :] < jnp.arange(tile_count)[:, None]
    position = jnp.sum(jnp.logical_and(matches, earlier), axis=1)
    slot_id = owners * capacity + position
    outbound = (
        jnp.zeros((risk_count * capacity, years_dev, TB), jnp.float32).at[slot_id].set(partials)
    )
    outbound = outbound.reshape(risk_count, capacity, years_dev, TB)
    sub_ids = (
        jnp.zeros((risk_count * capacity,), jnp.float32)
        .at[slot_id]
        .set(tile_sub.astype(jnp.float32))
    )
    sub_ids = sub_ids.reshape(risk_count, capacity)
    inbound, inbound_ids = (
        lax.all_to_all(outbound, "risk", split_axis=0, concat_axis=0, tiled=True),
        lax.all_to_all(sub_ids, "risk", split_axis=0, concat_axis=0, tiled=True),
    )
    selector = (
        inbound_ids.reshape(-1)[:, None] == jnp.arange(blocks_owned, dtype=jnp.float32)[None, :]
    ).astype(jnp.float32)
    gross = jnp.einsum(
        "sg,syb->ygb", selector, inbound.reshape(-1, years_dev, TB), precision=lax.Precision.HIGHEST
    )
    ceded = jnp.minimum(
        jnp.maximum(gross - attach.reshape(1, blocks_owned, TB), 0.0),
        limit.reshape(1, blocks_owned, TB),
    )
    ceded_low = ceded.astype(jnp.bfloat16)
    rein_blocks = REINS // RB
    selector_low = (
        share_rblock[:, :, None] == jnp.arange(rein_blocks, dtype=jnp.int32)[None, None, :]
    ).astype(jnp.bfloat16)
    shares = lax.all_gather(share_values, "tcol", axis=2, tiled=True)
    count_rows = shares.shape[2]
    spread = jnp.einsum("gkr,gktj->gtrj", selector_low, shares, preferred_element_type=jnp.float32)
    spread = spread.astype(jnp.bfloat16).reshape(blocks_owned, count_rows, REINS)
    retro_terms = jnp.einsum("ygt,gtr->yr", ceded_low, spread, preferred_element_type=jnp.float32)
    reinsurer_loss = lax.psum_scatter(retro_terms, "risk", scatter_dimension=1, tiled=True)
    return (ceded.reshape(years_dev, blocks_owned * TB), reinsurer_loss)


def solution(mesh):
    placed = (
        P("tcol", "risk"),
        P("tcol", None),
        P(None, "risk"),
        P("risk"),
        P("risk"),
        P("risk"),
        P("risk"),
        P("risk", None),
        P("risk"),
        P("risk"),
        P("risk"),
        P("risk", None, "tcol", None),
        P("risk", None),
    )
    dense = mesh.shape["risk"] == 4 * REINS // RB and mesh.shape["tcol"] == 2
    return jax.shard_map(
        dense_on_device if dense else sparse_on_device,
        mesh=mesh,
        in_specs=placed,
        out_specs=(P("tcol", "risk"), P("tcol", "risk")),
        check_vma=False,
    )
```

```python
import functools

import jax
import jax.numpy as jnp
from jax import lax
from jax.experimental import pallas as pl
from jax.experimental.pallas import tpu as pltpu
from jax.sharding import PartitionSpec as P

TB = 128
RB = 128
REINS = 512
TOP = 40.0
SCALE = 65535.0 / TOP
HALF = 32768
VMEM_SUMS = 56


def encode(sums):
    steps = jnp.minimum(sums * SCALE + 0.5, 65535.0).astype(jnp.int32) - HALF
    return steps.astype(jnp.int16)


def decode(*coded):
    return sum(a.astype(jnp.int32) + HALF for a in coded).astype(jnp.float32) * (1.0 / SCALE)


def add_coded(*coded):
    steps = sum(a.astype(jnp.int32) for a in coded) + (len(coded) - 1) * HALF
    return jnp.minimum(steps, HALF - 1).astype(jnp.int16)


def relative_code(rel, order):
    code = 0
    for bit in order:
        code = code * 2 + ((rel >> bit) & 1)
    return code


def block_sums_kernel(parts, owned, chunks, *refs):
    count = len(parts)
    in_refs, refs = refs[:9], refs[9:]
    send_refs, keep_refs, sum_refs, coded_refs = (refs[i * count : (i + 1) * count] for i in range(4))
    *held, small_sems, sems, out_sems = refs[4 * count :]
    owner_ref, sub_ref, factor_ref, scale_ref, sigma_ref, weight_ref, slot_ref, idio_ref, loads_ref = held
    half = keep_refs[0].shape[0]
    tiles = scale_ref.shape[0]
    per = tiles // chunks
    me = lax.axis_index("risk")
    core = lax.axis_index("tcol")

    def copies(i):
        cols = pl.ds(i * per * TB, per * TB)
        return [
            pltpu.make_async_copy(source.at[:, cols], target.at[:, cols], sems.at[j, i])
            for j, (source, target) in enumerate(zip(in_refs[7:], held[7:]))
        ]

    small = [
        pltpu.make_async_copy(source, target, small_sems.at[j])
        for j, (source, target) in enumerate(zip(in_refs[:7], held[:7]))
    ]
    for copy in small + [copy for i in range(chunks) for copy in copies(i)]:
        copy.start()
    for ref in sum_refs:
        ref[...] = jnp.zeros_like(ref)
    for copy in small:
        copy.wait()

    factor = factor_ref[...]
    rows = lax.broadcasted_iota(jnp.int32, (TB, TB), 0)

    for i in range(chunks):
        for copy in copies(i):
            copy.wait()
        for j in range(i * per, (i + 1) * per, GROUP):
            common = jnp.dot(factor, loads_ref[:, pl.ds(j * TB, GROUP * TB)], preferred_element_type=jnp.float32)
            group = []
            for k in range(j, j + GROUP):
                noise = idio_ref[:, pl.ds(k * TB, TB)].astype(jnp.float32)
                latent = common[:, (k - j) * TB : (k - j + 1) * TB] + weight_ref[pl.ds(k, 1), :] * noise
                losses = jnp.exp(scale_ref[pl.ds(k, 1), :] + sigma_ref[pl.ds(k, 1), :] * latent)
                group.append(losses.astype(jnp.bfloat16))
            for k, losses in zip(range(j, j + GROUP), group):
                chosen = (rows == slot_ref[pl.ds(k, 1), :]).astype(jnp.float32).astype(jnp.bfloat16)
                sums = lax.dot_general(
                    losses, chosen, (((1,), (1,)), ((), ())), preferred_element_type=jnp.float32
                )
                rel = owner_ref[k] ^ me
                for (first, years, order), sum_ref in zip(parts, sum_refs):
                    code = jnp.where(core == 0, relative_code(rel, order[0]), relative_code(rel, order[1]))
                    sum_ref[code * owned + sub_ref[k]] += sums[first : first + years]

    out = []
    piece = half // PIECES
    for i in range(PIECES):
        at = pl.ds(i * piece, piece)
        for p, (send_ref, keep_ref, sum_ref, coded_ref) in enumerate(zip(send_refs, keep_refs, sum_refs, coded_refs)):

            def body(b, carry):
                coded_ref[b] = encode(sum_ref[b])
                coded_ref[half + b] = encode(sum_ref[half + b])
                return carry

            lax.fori_loop(i * piece, (i + 1) * piece, body, 0, unroll=2)
            for j, (source, target) in enumerate(((coded_ref.at[pl.ds(half + i * piece, piece)], send_ref), (coded_ref.at[at], keep_ref))):
                copy = pltpu.make_async_copy(source, target.at[at], out_sems.at[p, i, j])
                copy.start()
                out.append(copy)
    for copy in out:
        copy.wait()


GROUP = 16
PIECES = 2


def block_sums(parts, idio, factor, loads, log_scale, sigma, weight, slot, owner, sub, blocks, owned, chunks=2):
    tiles = sub.shape[0]
    fold = lambda a: a.reshape(tiles, TB)
    hbm = pl.BlockSpec(memory_space=pltpu.HBM)
    shapes = [(blocks // 2, years, TB) for _, years, _ in parts]
    inputs = (owner.reshape(-1), sub, factor, fold(log_scale), fold(sigma), fold(weight), fold(slot), idio, loads)
    out = pl.pallas_call(
        functools.partial(block_sums_kernel, parts, owned, chunks),
        in_specs=[hbm] * len(inputs),
        out_specs=[hbm] * (2 * len(parts)),
        out_shape=[jax.ShapeDtypeStruct(s, jnp.int16) for s in shapes * 2],
        scratch_shapes=[pltpu.VMEM((blocks, years, TB), jnp.float32) for _, years, _ in parts]
        + [pltpu.VMEM((blocks, years, TB), jnp.int16) for _, years, _ in parts]
        + [pltpu.SMEM(a.shape, a.dtype) for a in inputs[:2]]
        + [pltpu.VMEM(a.shape, a.dtype) for a in inputs[2:]]
        + [
            pltpu.SemaphoreType.DMA((7,)),
            pltpu.SemaphoreType.DMA((2, chunks)),
            pltpu.SemaphoreType.DMA((len(parts), PIECES, 2)),
        ],
        compiler_params=pltpu.CompilerParams(vmem_limit_bytes=VMEM_SUMS * 2**20),
    )(*inputs)
    return out[: len(parts)], out[len(parts) :]


def retro_kernel(parts, rblock_ref, attach_ref, limit_ref, mine_ref, other_ref, *refs):
    *in_refs, ceded_ref, out_ref, acc_ref = refs
    each = len(in_refs) // len(parts)
    owned, tiles = mine_ref.shape[:2]
    first = lax.axis_index("tcol") == 0
    acc_ref[...] = jnp.zeros_like(acc_ref)
    for g in range(owned):
        sums = []
        for p in range(len(parts)):
            sums.append(decode(*(ref[g] for ref in in_refs[p * each : (p + 1) * each])))
        gross = jnp.concatenate(sums, axis=0)
        ceded = jnp.minimum(jnp.maximum(gross - attach_ref[pl.ds(g, 1), :], 0.0), limit_ref[pl.ds(g, 1), :])
        ceded_ref[:, pl.ds(g * TB, TB)] = ceded
        low = ceded.astype(jnp.bfloat16)
        for k in range(tiles):
            mine, other = mine_ref[g, k], other_ref[g, k]
            top = jnp.where(first, mine, other)
            bottom = jnp.where(first, other, mine)
            part = lax.dot_general(
                jnp.concatenate([top, bottom], axis=0), low, (((0,), (1,)), ((), ())),
                preferred_element_type=jnp.float32,
            )
            acc_ref[rblock_ref[g, k]] += part
    wide = RB // 4
    for q in range(acc_ref.shape[0]):
        for i in range(4):
            for h in range(2):
                out_ref[4 * q + i, :, h * 64 : (h + 1) * 64] = acc_ref[q, pl.ds(i * wide + h * wide // 2, wide // 2), :]


def retro(parts, inbound, attach, limit, mine, other, rblock):
    owned = mine.shape[0]
    years = sum(count for _, count, _ in parts)
    vmem = pl.BlockSpec(memory_space=pltpu.VMEM)
    whole = lambda a: pl.BlockSpec(a.shape, lambda i: (0,) * a.ndim)
    first = lambda a: pl.BlockSpec((owned,) + a.shape[1:], lambda i: (0, 0, 0))
    attach, limit = attach.reshape(owned, TB), limit.reshape(owned, TB)
    outs = [
        jax.ShapeDtypeStruct((years, owned * TB), jnp.float32),
        jax.ShapeDtypeStruct((REINS * 4 // RB, RB // 8, RB), jnp.float32),
    ]
    return pl.pallas_call(
        functools.partial(retro_kernel, parts),
        grid=(1,),
        in_specs=[pl.BlockSpec(memory_space=pltpu.SMEM)]
        + [whole(a) for a in (attach, limit, mine, other)]
        + [first(a) for a in inbound],
        out_specs=[whole(a) for a in outs],
        out_shape=outs,
        scratch_shapes=[pltpu.VMEM((REINS // RB, RB, years), jnp.float32)],
        compiler_params=pltpu.CompilerParams(vmem_limit_bytes=20 * 2**20),
    )(rblock, attach, limit, mine, other, *inbound)


def finish(pieces):
    years = pieces.shape[2] // 2
    return jnp.concatenate([jnp.sum(pieces[:, :, h * years : (h + 1) * years], axis=0) for h in range(2)], axis=0).T


PARTS = ((0, 16, ((0, 1, 2, 3), (1, 0, 2, 3))), (16, 16, ((0, 1, 2, 3), (1, 0, 2, 3))), (32, 16, ((0, 1, 2, 3), (1, 0, 2, 3))), (48, 16, ((2, 3, 0, 1), (2, 3, 1, 0))),)


def dense_on_device(
    idio_normals, factor_normals, loadings, log_scale, sigma, idio_weight, risk_slot,
    tile_owner, tile_sub, attach, limit, share_values, share_rblock,
):
    risk_count = lax.axis_size("risk")
    owned = attach.shape[0] // TB
    other_shares = lax.ppermute(share_values, "tcol", [(0, 1), (1, 0)])
    sends, keeps = block_sums(
        PARTS, idio_normals, factor_normals, loadings, log_scale, sigma, idio_weight, risk_slot,
        tile_owner, tile_sub, risk_count * owned, owned,
    )
    received = [[keep] for keep in keeps]
    sends = list(sends)
    steps = len(PARTS[0][2][0])
    count = keeps[0].shape[0]
    for step in range(steps):
        for p, (_, _, order) in enumerate(PARTS):
            pairs = [
                (2 * r + c, 2 * (r ^ (1 << order[c][step])) + c) for r in range(risk_count) for c in range(2)
            ]
            received[p].append(lax.ppermute(sends[p], ("risk", "tcol"), pairs))
        if step < steps - 1:
            count //= 2
            for p in range(len(PARTS)):
                sends[p] = add_coded(*(a[count : 2 * count] for a in received[p]))
    inbound = [a for arrays in received for a in arrays]
    ceded, pieces = retro(PARTS, inbound, attach, limit, share_values, other_shares, share_rblock)
    pieces = lax.all_to_all(pieces, "risk", split_axis=0, concat_axis=0, tiled=True)
    return ceded, finish(pieces)


def sparse_on_device(
    idio_normals, factor_normals, loadings, log_scale, sigma, idio_weight, risk_slot,
    tile_owner, tile_sub, attach, limit, share_values, share_rblock,
):
    risk_count = lax.axis_size("risk")
    years_dev, risk_dev = idio_normals.shape
    tile_count = tile_sub.shape[0]
    tile_rows = risk_dev // tile_count
    blocks_owned = attach.shape[0] // TB
    common = jnp.dot(factor_normals, loadings, preferred_element_type=jnp.float32)
    latent = common + idio_weight * idio_normals.astype(jnp.float32)
    losses = jnp.exp(log_scale + sigma * latent).astype(jnp.bfloat16)
    onehot = (
        risk_slot.reshape(tile_count, tile_rows)[:, :, None]
        == jnp.arange(TB, dtype=jnp.int32)[None, None, :]
    ).astype(jnp.bfloat16)
    partials = jnp.einsum(
        "ykr,krb->kyb",
        losses.reshape(years_dev, tile_count, tile_rows),
        onehot,
        preferred_element_type=jnp.float32,
    )
    owners = tile_owner[:, 0]
    capacity = 2 * tile_count // risk_count
    matches = owners[:, None] == owners[None, :]
    earlier = jnp.arange(tile_count)[None, :] < jnp.arange(tile_count)[:, None]
    position = jnp.sum(jnp.logical_and(matches, earlier), axis=1)
    slot_id = owners * capacity + position
    outbound = (
        jnp.zeros((risk_count * capacity, years_dev, TB), jnp.float32).at[slot_id].set(partials)
    )
    outbound = outbound.reshape(risk_count, capacity, years_dev, TB)
    sub_ids = (
        jnp.zeros((risk_count * capacity,), jnp.float32)
        .at[slot_id]
        .set(tile_sub.astype(jnp.float32))
    )
    sub_ids = sub_ids.reshape(risk_count, capacity)
    inbound, inbound_ids = (
        lax.all_to_all(outbound, "risk", split_axis=0, concat_axis=0, tiled=True),
        lax.all_to_all(sub_ids, "risk", split_axis=0, concat_axis=0, tiled=True),
    )
    selector = (
        inbound_ids.reshape(-1)[:, None] == jnp.arange(blocks_owned, dtype=jnp.float32)[None, :]
    ).astype(jnp.float32)
    gross = jnp.einsum(
        "sg,syb->ygb", selector, inbound.reshape(-1, years_dev, TB), precision=lax.Precision.HIGHEST
    )
    ceded = jnp.minimum(
        jnp.maximum(gross - attach.reshape(1, blocks_owned, TB), 0.0),
        limit.reshape(1, blocks_owned, TB),
    )
    ceded_low = ceded.astype(jnp.bfloat16)
    rein_blocks = REINS // RB
    selector_low = (
        share_rblock[:, :, None] == jnp.arange(rein_blocks, dtype=jnp.int32)[None, None, :]
    ).astype(jnp.bfloat16)
    shares = lax.all_gather(share_values, "tcol", axis=2, tiled=True)
    count_rows = shares.shape[2]
    spread = jnp.einsum("gkr,gktj->gtrj", selector_low, shares, preferred_element_type=jnp.float32)
    spread = spread.astype(jnp.bfloat16).reshape(blocks_owned, count_rows, REINS)
    retro_terms = jnp.einsum("ygt,gtr->yr", ceded_low, spread, preferred_element_type=jnp.float32)
    reinsurer_loss = lax.psum_scatter(retro_terms, "risk", scatter_dimension=1, tiled=True)
    return (ceded.reshape(years_dev, blocks_owned * TB), reinsurer_loss)


def solution(mesh):
    placed = (
        P("tcol", "risk"),
        P("tcol", None),
        P(None, "risk"),
        P("risk"),
        P("risk"),
        P("risk"),
        P("risk"),
        P("risk", None),
        P("risk"),
        P("risk"),
        P("risk"),
        P("risk", None, "tcol", None),
        P("risk", None),
    )
    dense = mesh.shape["risk"] == 4 * REINS // RB and mesh.shape["tcol"] == 2
    return jax.shard_map(
        dense_on_device if dense else sparse_on_device,
        mesh=mesh,
        in_specs=placed,
        out_specs=(P("tcol", "risk"), P("tcol", "risk")),
        check_vma=False,
    )
```

```python
import functools

import jax
import jax.numpy as jnp
from jax import lax
from jax.experimental import pallas as pl
from jax.experimental.pallas import tpu as pltpu
from jax.sharding import PartitionSpec as P

TB = 128
RB = 128
REINS = 512
TOP = 40.0
SCALE = 65535.0 / TOP
HALF = 32768
VMEM_SUMS = 24


def encode(sums):
    steps = jnp.minimum(sums * SCALE + 0.5, 65535.0).astype(jnp.int32) - HALF
    return steps.astype(jnp.int16)


def decode(*coded):
    return sum(a.astype(jnp.int32) + HALF for a in coded).astype(jnp.float32) * (1.0 / SCALE)


def add_coded(*coded):
    steps = sum(a.astype(jnp.int32) for a in coded) + (len(coded) - 1) * HALF
    return jnp.minimum(steps, HALF - 1).astype(jnp.int16)


def relative_code(rel, order):
    code = 0
    for bit in order:
        code = code * 2 + ((rel >> bit) & 1)
    return code


def block_sums_kernel(parts, owned, chunks, *refs):
    count = len(parts)
    in_refs, refs = refs[:9], refs[9:]
    send_refs, keep_refs, sum_refs = (refs[i * count : (i + 1) * count] for i in range(3))
    *held, small_sems, sems = refs[3 * count :]
    owner_ref, sub_ref, factor_ref, scale_ref, sigma_ref, weight_ref, slot_ref, idio_ref, loads_ref = held
    half = keep_refs[0].shape[0]
    tiles = scale_ref.shape[0]
    per = tiles // chunks
    me = lax.axis_index("risk")
    core = lax.axis_index("tcol")

    def copies(i):
        cols = pl.ds(i * per * TB, per * TB)
        return [
            pltpu.make_async_copy(source.at[:, cols], target.at[:, cols], sems.at[j, i])
            for j, (source, target) in enumerate(zip(in_refs[7:], held[7:]))
        ]

    small = [
        pltpu.make_async_copy(source, target, small_sems.at[j])
        for j, (source, target) in enumerate(zip(in_refs[:7], held[:7]))
    ]
    for copy in small + [copy for i in range(chunks) for copy in copies(i)]:
        copy.start()
    for ref in sum_refs:
        ref[...] = jnp.zeros_like(ref)
    for copy in small:
        copy.wait()

    factor = factor_ref[...]
    rows = lax.broadcasted_iota(jnp.int32, (TB, TB), 0)

    for i in range(chunks):
        for copy in copies(i):
            copy.wait()
        for j in range(i * per, (i + 1) * per, GROUP):
            common = jnp.dot(factor, loads_ref[:, pl.ds(j * TB, GROUP * TB)], preferred_element_type=jnp.float32)
            group = []
            for k in range(j, j + GROUP):
                noise = idio_ref[:, pl.ds(k * TB, TB)].astype(jnp.float32)
                latent = common[:, (k - j) * TB : (k - j + 1) * TB] + weight_ref[pl.ds(k, 1), :] * noise
                losses = jnp.exp(scale_ref[pl.ds(k, 1), :] + sigma_ref[pl.ds(k, 1), :] * latent)
                group.append(losses.astype(jnp.bfloat16))
            for k, losses in zip(range(j, j + GROUP), group):
                chosen = (rows == slot_ref[pl.ds(k, 1), :]).astype(jnp.float32).astype(jnp.bfloat16)
                sums = lax.dot_general(
                    losses, chosen, (((1,), (1,)), ((), ())), preferred_element_type=jnp.float32
                )
                rel = owner_ref[k] ^ me
                for (first, years, order), sum_ref in zip(parts, sum_refs):
                    code = jnp.where(core == 0, relative_code(rel, order[0]), relative_code(rel, order[1]))
                    sum_ref[code * owned + sub_ref[k]] += sums[first : first + years]

    for send_ref, keep_ref, sum_ref in zip(send_refs, keep_refs, sum_refs):

        def body(b, carry):
            send_ref[b] = encode(sum_ref[half + b])
            keep_ref[b] = encode(sum_ref[b])
            return carry

        lax.fori_loop(0, half, body, 0, unroll=4)


GROUP = 16


def block_sums(parts, idio, factor, loads, log_scale, sigma, weight, slot, owner, sub, blocks, owned, chunks=2):
    tiles = sub.shape[0]
    fold = lambda a: a.reshape(tiles, TB)
    hbm = pl.BlockSpec(memory_space=pltpu.HBM)
    shapes = [(blocks // 2, years, TB) for _, years, _ in parts]
    inputs = (owner.reshape(-1), sub, factor, fold(log_scale), fold(sigma), fold(weight), fold(slot), idio, loads)
    out = pl.pallas_call(
        functools.partial(block_sums_kernel, parts, owned, chunks),
        in_specs=[hbm] * len(inputs),
        out_specs=[pl.BlockSpec(memory_space=pltpu.VMEM)] * (2 * len(parts)),
        out_shape=[jax.ShapeDtypeStruct(s, jnp.int16) for s in shapes * 2],
        scratch_shapes=[pltpu.VMEM((blocks, years, TB), jnp.float32) for _, years, _ in parts]
        + [pltpu.SMEM(a.shape, a.dtype) for a in inputs[:2]]
        + [pltpu.VMEM(a.shape, a.dtype) for a in inputs[2:]]
        + [
            pltpu.SemaphoreType.DMA((7,)),
            pltpu.SemaphoreType.DMA((2, chunks)),
        ],
        compiler_params=pltpu.CompilerParams(vmem_limit_bytes=VMEM_SUMS * 2**20),
    )(*(pltpu.with_memory_space_constraint(a, pltpu.HBM) for a in inputs))
    return out[: len(parts)], out[len(parts) :]


def retro_kernel(parts, rblock_ref, attach_ref, limit_ref, mine_ref, other_ref, *refs):
    *in_refs, ceded_ref, out_ref, acc_ref = refs
    each = len(in_refs) // len(parts)
    owned, tiles = mine_ref.shape[:2]
    first = lax.axis_index("tcol") == 0
    acc_ref[...] = jnp.zeros_like(acc_ref)
    for g in range(owned):
        sums = []
        for p in range(len(parts)):
            sums.append(decode(*(ref[g] for ref in in_refs[p * each : (p + 1) * each])))
        gross = jnp.concatenate(sums, axis=0)
        ceded = jnp.minimum(jnp.maximum(gross - attach_ref[pl.ds(g, 1), :], 0.0), limit_ref[pl.ds(g, 1), :])
        ceded_ref[:, pl.ds(g * TB, TB)] = ceded
        low = ceded.astype(jnp.bfloat16)
        for k in range(tiles):
            mine, other = mine_ref[g, k], other_ref[g, k]
            top = jnp.where(first, mine, other)
            bottom = jnp.where(first, other, mine)
            part = lax.dot_general(
                jnp.concatenate([top, bottom], axis=0), low, (((0,), (1,)), ((), ())),
                preferred_element_type=jnp.float32,
            )
            acc_ref[rblock_ref[g, k]] += part
    wide = RB // 4
    for q in range(acc_ref.shape[0]):
        for i in range(4):
            for h in range(2):
                out_ref[4 * q + i, :, h * 64 : (h + 1) * 64] = acc_ref[q, pl.ds(i * wide + h * wide // 2, wide // 2), :]


def retro(parts, inbound, attach, limit, mine, other, rblock):
    owned = mine.shape[0]
    years = sum(count for _, count, _ in parts)
    vmem = pl.BlockSpec(memory_space=pltpu.VMEM)
    whole = lambda a: pl.BlockSpec(a.shape, lambda i: (0,) * a.ndim)
    first = lambda a: pl.BlockSpec((owned,) + a.shape[1:], lambda i: (0, 0, 0))
    attach, limit = attach.reshape(owned, TB), limit.reshape(owned, TB)
    outs = [
        jax.ShapeDtypeStruct((years, owned * TB), jnp.float32),
        jax.ShapeDtypeStruct((REINS * 4 // RB, RB // 8, RB), jnp.float32),
    ]
    return pl.pallas_call(
        functools.partial(retro_kernel, parts),
        grid=(1,),
        in_specs=[pl.BlockSpec(memory_space=pltpu.SMEM)]
        + [whole(a) for a in (attach, limit, mine, other)]
        + [first(a) for a in inbound],
        out_specs=[whole(a) for a in outs],
        out_shape=outs,
        scratch_shapes=[pltpu.VMEM((REINS // RB, RB, years), jnp.float32)],
        compiler_params=pltpu.CompilerParams(vmem_limit_bytes=20 * 2**20),
    )(rblock, attach, limit, mine, other, *inbound)


def finish(pieces):
    years = pieces.shape[2] // 2
    return jnp.concatenate([jnp.sum(pieces[:, :, h * years : (h + 1) * years], axis=0) for h in range(2)], axis=0).T


PARTS = ((0, 32, ((0, 1, 2, 3), (1, 0, 2, 3))), (32, 16, ((0, 1, 2, 3), (1, 0, 2, 3))), (48, 16, ((2, 3, 0, 1), (2, 3, 1, 0))),)


def dense_on_device(
    idio_normals, factor_normals, loadings, log_scale, sigma, idio_weight, risk_slot,
    tile_owner, tile_sub, attach, limit, share_values, share_rblock,
):
    risk_count = lax.axis_size("risk")
    owned = attach.shape[0] // TB
    other_shares = lax.ppermute(share_values, "tcol", [(0, 1), (1, 0)])
    sends, keeps = block_sums(
        PARTS, idio_normals, factor_normals, loadings, log_scale, sigma, idio_weight, risk_slot,
        tile_owner, tile_sub, risk_count * owned, owned,
    )
    received = [[keep] for keep in keeps]
    sends = list(sends)
    steps = len(PARTS[0][2][0])
    count = keeps[0].shape[0]
    for step in range(steps):
        for p, (_, _, order) in enumerate(PARTS):
            pairs = [
                (2 * r + c, 2 * (r ^ (1 << order[c][step])) + c) for r in range(risk_count) for c in range(2)
            ]
            received[p].append(lax.ppermute(sends[p], ("risk", "tcol"), pairs))
        if step < steps - 1:
            count //= 2
            for p in range(len(PARTS)):
                sends[p] = add_coded(*(a[count : 2 * count] for a in received[p]))
    inbound = [a for arrays in received for a in arrays]
    ceded, pieces = retro(PARTS, inbound, attach, limit, share_values, other_shares, share_rblock)
    pieces = lax.all_to_all(pieces, "risk", split_axis=0, concat_axis=0, tiled=True)
    return ceded, finish(pieces)


def sparse_on_device(
    idio_normals, factor_normals, loadings, log_scale, sigma, idio_weight, risk_slot,
    tile_owner, tile_sub, attach, limit, share_values, share_rblock,
):
    risk_count = lax.axis_size("risk")
    years_dev, risk_dev = idio_normals.shape
    tile_count = tile_sub.shape[0]
    tile_rows = risk_dev // tile_count
    blocks_owned = attach.shape[0] // TB
    common = jnp.dot(factor_normals, loadings, preferred_element_type=jnp.float32)
    latent = common + idio_weight * idio_normals.astype(jnp.float32)
    losses = jnp.exp(log_scale + sigma * latent).astype(jnp.bfloat16)
    onehot = (
        risk_slot.reshape(tile_count, tile_rows)[:, :, None]
        == jnp.arange(TB, dtype=jnp.int32)[None, None, :]
    ).astype(jnp.bfloat16)
    partials = jnp.einsum(
        "ykr,krb->kyb",
        losses.reshape(years_dev, tile_count, tile_rows),
        onehot,
        preferred_element_type=jnp.float32,
    )
    owners = tile_owner[:, 0]
    capacity = 2 * tile_count // risk_count
    matches = owners[:, None] == owners[None, :]
    earlier = jnp.arange(tile_count)[None, :] < jnp.arange(tile_count)[:, None]
    position = jnp.sum(jnp.logical_and(matches, earlier), axis=1)
    slot_id = owners * capacity + position
    outbound = (
        jnp.zeros((risk_count * capacity, years_dev, TB), jnp.float32).at[slot_id].set(partials)
    )
    outbound = outbound.reshape(risk_count, capacity, years_dev, TB)
    sub_ids = (
        jnp.zeros((risk_count * capacity,), jnp.float32)
        .at[slot_id]
        .set(tile_sub.astype(jnp.float32))
    )
    sub_ids = sub_ids.reshape(risk_count, capacity)
    inbound, inbound_ids = (
        lax.all_to_all(outbound, "risk", split_axis=0, concat_axis=0, tiled=True),
        lax.all_to_all(sub_ids, "risk", split_axis=0, concat_axis=0, tiled=True),
    )
    selector = (
        inbound_ids.reshape(-1)[:, None] == jnp.arange(blocks_owned, dtype=jnp.float32)[None, :]
    ).astype(jnp.float32)
    gross = jnp.einsum(
        "sg,syb->ygb", selector, inbound.reshape(-1, years_dev, TB), precision=lax.Precision.HIGHEST
    )
    ceded = jnp.minimum(
        jnp.maximum(gross - attach.reshape(1, blocks_owned, TB), 0.0),
        limit.reshape(1, blocks_owned, TB),
    )
    ceded_low = ceded.astype(jnp.bfloat16)
    rein_blocks = REINS // RB
    selector_low = (
        share_rblock[:, :, None] == jnp.arange(rein_blocks, dtype=jnp.int32)[None, None, :]
    ).astype(jnp.bfloat16)
    shares = lax.all_gather(share_values, "tcol", axis=2, tiled=True)
    count_rows = shares.shape[2]
    spread = jnp.einsum("gkr,gktj->gtrj", selector_low, shares, preferred_element_type=jnp.float32)
    spread = spread.astype(jnp.bfloat16).reshape(blocks_owned, count_rows, REINS)
    retro_terms = jnp.einsum("ygt,gtr->yr", ceded_low, spread, preferred_element_type=jnp.float32)
    reinsurer_loss = lax.psum_scatter(retro_terms, "risk", scatter_dimension=1, tiled=True)
    return (ceded.reshape(years_dev, blocks_owned * TB), reinsurer_loss)


def solution(mesh):
    placed = (
        P("tcol", "risk"),
        P("tcol", None),
        P(None, "risk"),
        P("risk"),
        P("risk"),
        P("risk"),
        P("risk"),
        P("risk", None),
        P("risk"),
        P("risk"),
        P("risk"),
        P("risk", None, "tcol", None),
        P("risk", None),
    )
    dense = mesh.shape["risk"] == 4 * REINS // RB and mesh.shape["tcol"] == 2
    return jax.shard_map(
        dense_on_device if dense else sparse_on_device,
        mesh=mesh,
        in_specs=placed,
        out_specs=(P("tcol", "risk"), P("tcol", "risk")),
        check_vma=False,
    )
```

```python
import functools

import jax
import jax.numpy as jnp
from jax import lax
from jax.experimental import pallas as pl
from jax.experimental.pallas import tpu as pltpu
from jax.sharding import PartitionSpec as P

TB = 128
RB = 128
REINS = 512
TOP = 40.0
SCALE = 65535.0 / TOP
HALF = 32768
VMEM_SUMS = 24


def encode(sums):
    steps = jnp.minimum(sums * SCALE + 0.5, 65535.0).astype(jnp.int32) - HALF
    return steps.astype(jnp.int16)


def decode(*coded):
    return sum(a.astype(jnp.int32) + HALF for a in coded).astype(jnp.float32) * (1.0 / SCALE)


def add_coded(*coded):
    steps = sum(a.astype(jnp.int32) for a in coded) + (len(coded) - 1) * HALF
    return jnp.minimum(steps, HALF - 1).astype(jnp.int16)


def relative_code(rel, order):
    code = 0
    for bit in order:
        code = code * 2 + ((rel >> bit) & 1)
    return code


def block_sums_kernel(parts, owned, chunks, *refs):
    count = len(parts)
    in_refs, refs = refs[:9], refs[9:]
    send_refs, keep_refs, sum_refs = (refs[i * count : (i + 1) * count] for i in range(3))
    *held, small_sems, sems = refs[3 * count :]
    owner_ref, sub_ref, factor_ref, scale_ref, sigma_ref, weight_ref, slot_ref, idio_ref, loads_ref = held
    half = keep_refs[0].shape[0]
    tiles = scale_ref.shape[0]
    per = tiles // chunks
    me = lax.axis_index("risk")
    core = lax.axis_index("tcol")

    def copies(i):
        cols = pl.ds(i * per * TB, per * TB)
        return [
            pltpu.make_async_copy(source.at[:, cols], target.at[:, cols], sems.at[j, i])
            for j, (source, target) in enumerate(zip(in_refs[7:], held[7:]))
        ]

    small = [
        pltpu.make_async_copy(source, target, small_sems.at[j])
        for j, (source, target) in enumerate(zip(in_refs[:7], held[:7]))
    ]
    for copy in small + [copy for i in range(chunks) for copy in copies(i)]:
        copy.start()
    for ref in sum_refs:
        ref[...] = jnp.zeros_like(ref)
    for copy in small:
        copy.wait()

    factor = factor_ref[...]
    rows = lax.broadcasted_iota(jnp.int32, (TB, TB), 0)

    for i in range(chunks):
        for copy in copies(i):
            copy.wait()
        for j in range(i * per, (i + 1) * per, GROUP):
            common = jnp.dot(factor, loads_ref[:, pl.ds(j * TB, GROUP * TB)], preferred_element_type=jnp.float32)
            group = []
            for k in range(j, j + GROUP):
                noise = idio_ref[:, pl.ds(k * TB, TB)].astype(jnp.float32)
                latent = common[:, (k - j) * TB : (k - j + 1) * TB] + weight_ref[pl.ds(k, 1), :] * noise
                losses = jnp.exp(scale_ref[pl.ds(k, 1), :] + sigma_ref[pl.ds(k, 1), :] * latent)
                group.append(losses.astype(jnp.bfloat16))
            for k, losses in zip(range(j, j + GROUP), group):
                chosen = (rows == slot_ref[pl.ds(k, 1), :]).astype(jnp.float32).astype(jnp.bfloat16)
                sums = lax.dot_general(
                    losses, chosen, (((1,), (1,)), ((), ())), preferred_element_type=jnp.float32
                )
                rel = owner_ref[k] ^ me
                for (first, years, order), sum_ref in zip(parts, sum_refs):
                    code = jnp.where(core == 0, relative_code(rel, order[0]), relative_code(rel, order[1]))
                    sum_ref[code * owned + sub_ref[k]] += sums[first : first + years]

    for send_ref, keep_ref, sum_ref in zip(send_refs, keep_refs, sum_refs):

        def body(b, carry):
            send_ref[b] = encode(sum_ref[half + b])
            keep_ref[b] = encode(sum_ref[b])
            return carry

        lax.fori_loop(0, half, body, 0, unroll=4)


GROUP = 16


def block_sums(parts, idio, factor, loads, log_scale, sigma, weight, slot, owner, sub, blocks, owned, chunks=2):
    tiles = sub.shape[0]
    fold = lambda a: a.reshape(tiles, TB)
    hbm = pl.BlockSpec(memory_space=pltpu.HBM)
    shapes = [(blocks // 2, years, TB) for _, years, _ in parts]
    inputs = (owner.reshape(-1), sub, factor, fold(log_scale), fold(sigma), fold(weight), fold(slot), idio, loads)
    out = pl.pallas_call(
        functools.partial(block_sums_kernel, parts, owned, chunks),
        in_specs=[hbm] * len(inputs),
        out_specs=[pl.BlockSpec(memory_space=pltpu.VMEM)] * (2 * len(parts)),
        out_shape=[jax.ShapeDtypeStruct(s, jnp.int16) for s in shapes * 2],
        scratch_shapes=[pltpu.VMEM((blocks, years, TB), jnp.float32) for _, years, _ in parts]
        + [pltpu.SMEM(a.shape, a.dtype) for a in inputs[:2]]
        + [pltpu.VMEM(a.shape, a.dtype) for a in inputs[2:]]
        + [
            pltpu.SemaphoreType.DMA((7,)),
            pltpu.SemaphoreType.DMA((2, chunks)),
        ],
        compiler_params=pltpu.CompilerParams(vmem_limit_bytes=VMEM_SUMS * 2**20),
    )(*(pltpu.with_memory_space_constraint(a, pltpu.HBM) for a in inputs))
    return out[: len(parts)], out[len(parts) :]


def retro_kernel(parts, rblock_ref, attach_ref, limit_ref, mine_ref, other_ref, *refs):
    *in_refs, ceded_ref, out_ref, acc_ref = refs
    each = len(in_refs) // len(parts)
    owned, tiles = mine_ref.shape[:2]
    first = lax.axis_index("tcol") == 0
    acc_ref[...] = jnp.zeros_like(acc_ref)
    for g in range(owned):
        sums = []
        for p in range(len(parts)):
            sums.append(decode(*(ref[g] for ref in in_refs[p * each : (p + 1) * each])))
        gross = jnp.concatenate(sums, axis=0)
        ceded = jnp.minimum(jnp.maximum(gross - attach_ref[pl.ds(g, 1), :], 0.0), limit_ref[pl.ds(g, 1), :])
        ceded_ref[:, pl.ds(g * TB, TB)] = ceded
        low = ceded.astype(jnp.bfloat16)
        for k in range(tiles):
            mine, other = mine_ref[g, k], other_ref[g, k]
            top = jnp.where(first, mine, other)
            bottom = jnp.where(first, other, mine)
            part = jnp.dot(low, jnp.concatenate([top, bottom], axis=0), preferred_element_type=jnp.float32)
            acc_ref[rblock_ref[g, k]] += part
    wide = RB // 4
    for q in range(acc_ref.shape[0]):
        turned = acc_ref[q].T
        for i in range(4):
            for h in range(2):
                out_ref[4 * q + i, :, h * 64 : (h + 1) * 64] = turned[i * wide + h * wide // 2 : i * wide + (h + 1) * wide // 2]


def retro(parts, inbound, attach, limit, mine, other, rblock):
    owned = mine.shape[0]
    years = sum(count for _, count, _ in parts)
    vmem = pl.BlockSpec(memory_space=pltpu.VMEM)
    whole = lambda a: pl.BlockSpec(a.shape, lambda i: (0,) * a.ndim)
    first = lambda a: pl.BlockSpec((owned,) + a.shape[1:], lambda i: (0, 0, 0))
    attach, limit = attach.reshape(owned, TB), limit.reshape(owned, TB)
    outs = [
        jax.ShapeDtypeStruct((years, owned * TB), jnp.float32),
        jax.ShapeDtypeStruct((REINS * 4 // RB, RB // 8, RB), jnp.float32),
    ]
    return pl.pallas_call(
        functools.partial(retro_kernel, parts),
        grid=(1,),
        in_specs=[pl.BlockSpec(memory_space=pltpu.SMEM)]
        + [whole(a) for a in (attach, limit, mine, other)]
        + [first(a) for a in inbound],
        out_specs=[whole(a) for a in outs],
        out_shape=outs,
        scratch_shapes=[pltpu.VMEM((REINS // RB, years, RB), jnp.float32)],
        compiler_params=pltpu.CompilerParams(vmem_limit_bytes=20 * 2**20),
    )(rblock, attach, limit, mine, other, *inbound)


def finish(pieces):
    years = pieces.shape[2] // 2
    return jnp.concatenate([jnp.sum(pieces[:, :, h * years : (h + 1) * years], axis=0) for h in range(2)], axis=0).T


PARTS = (
    (0, 16, ((2, 3, 0, 1), (2, 3, 1, 0))),
    (16, 16, ((0, 1, 2, 3), (1, 0, 2, 3))),
    (32, 16, ((1, 0, 2, 3), (0, 1, 2, 3))),
    (48, 16, ((1, 0, 2, 3), (0, 1, 2, 3))),
)


def dense_on_device(
    idio_normals, factor_normals, loadings, log_scale, sigma, idio_weight, risk_slot,
    tile_owner, tile_sub, attach, limit, share_values, share_rblock,
):
    risk_count = lax.axis_size("risk")
    owned = attach.shape[0] // TB
    other_shares = lax.ppermute(share_values, "tcol", [(0, 1), (1, 0)])
    sends, keeps = block_sums(
        PARTS, idio_normals, factor_normals, loadings, log_scale, sigma, idio_weight, risk_slot,
        tile_owner, tile_sub, risk_count * owned, owned,
    )
    received = [[keep] for keep in keeps]
    sends = list(sends)
    steps = len(PARTS[0][2][0])
    count = keeps[0].shape[0]
    for step in range(steps):
        for p, (_, _, order) in enumerate(PARTS):
            pairs = [
                (2 * r + c, 2 * (r ^ (1 << order[c][step])) + c) for r in range(risk_count) for c in range(2)
            ]
            received[p].append(lax.ppermute(sends[p], ("risk", "tcol"), pairs))
        if step < steps - 1:
            count //= 2
            for p in range(len(PARTS)):
                sends[p] = add_coded(*(a[count : 2 * count] for a in received[p]))
    inbound = [a for arrays in received for a in arrays]
    ceded, pieces = retro(PARTS, inbound, attach, limit, share_values, other_shares, share_rblock)
    pieces = lax.all_to_all(pieces, "risk", split_axis=0, concat_axis=0, tiled=True)
    return ceded, finish(pieces)


def sparse_on_device(
    idio_normals, factor_normals, loadings, log_scale, sigma, idio_weight, risk_slot,
    tile_owner, tile_sub, attach, limit, share_values, share_rblock,
):
    risk_count = lax.axis_size("risk")
    years_dev, risk_dev = idio_normals.shape
    tile_count = tile_sub.shape[0]
    tile_rows = risk_dev // tile_count
    blocks_owned = attach.shape[0] // TB
    common = jnp.dot(factor_normals, loadings, preferred_element_type=jnp.float32)
    latent = common + idio_weight * idio_normals.astype(jnp.float32)
    losses = jnp.exp(log_scale + sigma * latent).astype(jnp.bfloat16)
    onehot = (
        risk_slot.reshape(tile_count, tile_rows)[:, :, None]
        == jnp.arange(TB, dtype=jnp.int32)[None, None, :]
    ).astype(jnp.bfloat16)
    partials = jnp.einsum(
        "ykr,krb->kyb",
        losses.reshape(years_dev, tile_count, tile_rows),
        onehot,
        preferred_element_type=jnp.float32,
    )
    owners = tile_owner[:, 0]
    capacity = 2 * tile_count // risk_count
    matches = owners[:, None] == owners[None, :]
    earlier = jnp.arange(tile_count)[None, :] < jnp.arange(tile_count)[:, None]
    position = jnp.sum(jnp.logical_and(matches, earlier), axis=1)
    slot_id = owners * capacity + position
    outbound = (
        jnp.zeros((risk_count * capacity, years_dev, TB), jnp.float32).at[slot_id].set(partials)
    )
    outbound = outbound.reshape(risk_count, capacity, years_dev, TB)
    sub_ids = (
        jnp.zeros((risk_count * capacity,), jnp.float32)
        .at[slot_id]
        .set(tile_sub.astype(jnp.float32))
    )
    sub_ids = sub_ids.reshape(risk_count, capacity)
    inbound, inbound_ids = (
        lax.all_to_all(outbound, "risk", split_axis=0, concat_axis=0, tiled=True),
        lax.all_to_all(sub_ids, "risk", split_axis=0, concat_axis=0, tiled=True),
    )
    selector = (
        inbound_ids.reshape(-1)[:, None] == jnp.arange(blocks_owned, dtype=jnp.float32)[None, :]
    ).astype(jnp.float32)
    gross = jnp.einsum(
        "sg,syb->ygb", selector, inbound.reshape(-1, years_dev, TB), precision=lax.Precision.HIGHEST
    )
    ceded = jnp.minimum(
        jnp.maximum(gross - attach.reshape(1, blocks_owned, TB), 0.0),
        limit.reshape(1, blocks_owned, TB),
    )
    ceded_low = ceded.astype(jnp.bfloat16)
    rein_blocks = REINS // RB
    selector_low = (
        share_rblock[:, :, None] == jnp.arange(rein_blocks, dtype=jnp.int32)[None, None, :]
    ).astype(jnp.bfloat16)
    shares = lax.all_gather(share_values, "tcol", axis=2, tiled=True)
    count_rows = shares.shape[2]
    spread = jnp.einsum("gkr,gktj->gtrj", selector_low, shares, preferred_element_type=jnp.float32)
    spread = spread.astype(jnp.bfloat16).reshape(blocks_owned, count_rows, REINS)
    retro_terms = jnp.einsum("ygt,gtr->yr", ceded_low, spread, preferred_element_type=jnp.float32)
    reinsurer_loss = lax.psum_scatter(retro_terms, "risk", scatter_dimension=1, tiled=True)
    return (ceded.reshape(years_dev, blocks_owned * TB), reinsurer_loss)


def solution(mesh):
    placed = (
        P("tcol", "risk"),
        P("tcol", None),
        P(None, "risk"),
        P("risk"),
        P("risk"),
        P("risk"),
        P("risk"),
        P("risk", None),
        P("risk"),
        P("risk"),
        P("risk"),
        P("risk", None, "tcol", None),
        P("risk", None),
    )
    dense = mesh.shape["risk"] == 4 * REINS // RB and mesh.shape["tcol"] == 2
    return jax.shard_map(
        dense_on_device if dense else sparse_on_device,
        mesh=mesh,
        in_specs=placed,
        out_specs=(P("tcol", "risk"), P("tcol", "risk")),
        check_vma=False,
    )
```
